128 devices in a mesh: pipe: 8 (over y_lo, z), expert: 16 (over x, y_hi, core).
Axes of the slice: x: 4, y: 4 (y_hi: 2, y_lo: 2; y = y_hi * 2 + y_lo), z: 4, core: 2. Of those that a mesh axis runs over, the one named last changes fastest.
Arguments:
- out_grad: bfloat16 [8, 2, 1024, 3584], P('pipe', None, 'expert'), may hold values from -6 to 6
- saved_input: bfloat16 [8, 2, 1024, 3584], P('pipe', None, 'expert'), may hold values from -6 to 6
- saved_hidden: bfloat16 [8, 2, 1024, 8, 1024], P('pipe', None, 'expert'), may hold values from -0.29882812 to 0.29882812
- expert_ids: int32 [8, 2, 1024, 8], P('pipe', None, 'expert'), may hold values from 0 to 15, all different within a row; in each aligned block of 64 rows (0 to 63, 64 to 127, ..., all dimensions but the last counted through in order) at most 56 rows name the same one
- down_weight: bfloat16 [8, 2, 16, 1024, 3584], P('pipe', None, 'expert'), may hold values from -0.1875 to 0.1875
- router_weight: bfloat16 [8, 2, 16, 3584], P('pipe'), may hold values from -0.09375 to 0.09375
Outputs:
- hidden_grad: bfloat16 [8, 2, 1024, 8, 1024], P('pipe', None, 'expert')
- router_grad: float32 [8, 2, 16, 3584], P('pipe')
The draws below stay inside these ranges and needn't reach their ends.
Inputs may be any that keep to these rules, and one draw needn't show every extreme that they name: `expert_ids`: each token names 8 different experts. Among the 64 tokens of one device in one slot, no expert is named by more than 56, and in some of these blocks one is named by exactly 56.
All inputs are finite; a program needn't handle non-finite values.
Results may differ from the reference program's by a relative error of at most 0.005.
Values may be sent and summed in bfloat16 or wider, within the bound.
No kernel may reach another device: no remote copies, remote signals or barrier semaphores. Data moves between devices by JAX's collectives and lax.ppermute only.
A program may use at most 128 MiB of HBM per device.

```python
import math
import jax
import jax.numpy as jnp
import numpy as np
from jax import lax

DW = 3584
HID = 1024
TOK_DEV = 64
CAP = 56
EXPERTS = 16
TOPK = 8
TOKENS = 1024
N_PIPE = 8


def block_scale(own_key, dims, shards, least, top_value):
    def one(position, parts):
        draws = jax.random.uniform(jax.random.fold_in(jax.random.fold_in(own_key, 6), position), (parts,), jnp.float32, least / len(shards), top_value / len(shards))
        return jnp.repeat(jnp.exp(draws), dims[position] // parts).reshape((-1,) + (1,) * (len(dims) - position - 1))

    factor_of = one(*shards[0])
    for cut in shards[1:]:
        factor_of = factor_of * one(*cut)
    return factor_of


def routed_block(own_key, own, number, rows, count, top, most, slope):
    ranking = jax.random.permutation(own_key, count)
    packed, common = load_shares(count, rows * top, most, slope, True), load_shares(count, rows * top, most, slope, False)
    places = jnp.arange(count)

    def named(sizes, rotation):
        used = int((sizes > 0).sum())
        fixed = max(1, used // 4)
        passed = fixed + (places - fixed + rotation * (used - fixed)) % max(1, count - fixed)
        return jnp.zeros((count,), jnp.int32).at[ranking[jnp.where(places < fixed, places, passed)]].set(jnp.asarray(sizes, jnp.int32))

    sizes = jnp.where(number % 4 == 0, named(packed, number // 4), named(common, number - number // 4 - 1))
    mixed = jax.random.permutation(jax.random.fold_in(own, 3), count)
    source_of, sink = mixed[0:count // 2 * 2:2], mixed[1:count // 2 * 2:2]
    slack = jnp.minimum(sizes[source_of] - 1, most - sizes[sink]) // 2
    slack = jnp.where((source_of == ranking[0]) | (sink == ranking[0]) | (sizes[sink] == 0), 0, jnp.maximum(slack, 0))
    passed = jax.random.randint(jax.random.fold_in(own, 4), (count // 2,), 0, 1 << 20) % (slack + 1)
    sizes = sizes.at[source_of].add(-passed).at[sink].add(passed)
    items = jnp.searchsorted(jnp.cumsum(sizes), jnp.arange(rows * top), side="right").astype(jnp.int32)
    listing = items.reshape(top, rows).T
    listing = listing[jax.random.permutation(jax.random.fold_in(own, 1), rows)]
    rotation = jax.random.randint(jax.random.fold_in(own, 2), (rows, 1), 0, top)
    return jnp.take_along_axis(listing, (jnp.arange(top)[None, :] + rotation) % top, axis=1)


def load_shares(count, total, bound, skew, full):
    weights = [(1 << 20) // math.isqrt(grade ** skew) + 1 for grade in range(1, count + 1)]
    largest = bound if full else min(bound, max(-(-total // count), total * weights[0] // sum(weights)))
    least = 1 if total - largest >= count - 1 else 0
    holding, rest = [largest] + [least] * (count - 1), total - largest - least * (count - 1)
    while rest > 0:
        candidates = [i for i in range(1, count) if holding[i] < largest] or [i for i in range(1, count) if holding[i] < bound]
        whole, budget = sum([weights[i] for i in candidates]), rest
        for i in candidates:
            addition = min(bound - holding[i], max(1, budget * weights[i] // whole), rest)
            holding[i] = holding[i] + addition
            rest = rest - addition
    return np.array(holding)


def noise(own_key, shape, scale, most, pieces=(), held_as=jnp.bfloat16):
    level = block_scale(own_key, shape, pieces, -0.22, 0.18) if pieces else 1.0
    drawn = jax.random.normal(own_key, shape, jnp.float32) * scale * level
    return jnp.minimum(jnp.maximum(drawn, -most), most).astype(held_as)


def setup_inputs(seed: int = 0) -> dict:
    arg_keys = jax.random.split(jax.random.key(seed), 7)
    out_grad = noise(arg_keys[0], (N_PIPE, 2, TOKENS, DW), 1.0, 6.0, ((0, 8), (2, 16)))
    saved_input = noise(arg_keys[1], (N_PIPE, 2, TOKENS, DW), 1.0, 6.0, ((0, 8), (2, 16)))
    saved_hidden = noise(arg_keys[2], (N_PIPE, 2, TOKENS, TOPK, HID), 0.05, 0.29882812, ((0, 8), (2, 16)))
    expert_ids_keys = jax.random.split(jax.random.fold_in(arg_keys[3], 1), N_PIPE * 2 * TOKENS // TOK_DEV)
    expert_ids_turns = jax.random.permutation(jax.random.fold_in(arg_keys[3], 3), N_PIPE * 2 * TOKENS // TOK_DEV)
    expert_ids = jax.vmap(lambda own, number: routed_block(jax.random.fold_in(arg_keys[3], 2), own, number, TOK_DEV, EXPERTS, TOPK, CAP, 2))(expert_ids_keys, expert_ids_turns).reshape((N_PIPE, 2, TOKENS, TOPK))
    down_weight = noise(arg_keys[4], (N_PIPE, 2, EXPERTS, HID, DW), HID ** -0.5, 0.1875, ((0, 8), (2, 16)))
    router_weight = noise(arg_keys[5], (N_PIPE, 2, EXPERTS, DW), DW ** -0.5, 0.09375, ((0, 8),))
    return {"out_grad": out_grad, "saved_input": saved_input, "saved_hidden": saved_hidden, "expert_ids": expert_ids, "down_weight": down_weight, "router_weight": router_weight}


route_scale = 2.5


def token_math(back, hidden, inputs, routes, router):
    member = routes[:, :, None] == jnp.arange(EXPERTS, dtype=jnp.int32)[None, None, :]
    dgate = jnp.sum(hidden.astype(jnp.float32) * back.astype(jnp.float32), axis=2)
    logits = jnp.dot(inputs, router.T, preferred_element_type=jnp.float32)
    probs = jax.nn.sigmoid(logits)
    chosen = jnp.sum(jnp.where(member, probs[:, None, :], 0.0), axis=2)
    total = jnp.sum(chosen, axis=1, keepdims=True)
    weights = route_scale * chosen / total
    hidden_grad = (weights[:, :, None] * back.astype(jnp.float32)).astype(jnp.bfloat16)
    centred = dgate - jnp.sum(chosen / total * dgate, axis=1, keepdims=True)
    selected = route_scale / total * centred * chosen * (1.0 - chosen)
    logit_grad = jnp.sum(jnp.where(member, selected[:, :, None], 0.0), axis=1)
    partial_value = jnp.dot(logit_grad.T, inputs.astype(jnp.float32), precision=lax.Precision.HIGHEST)
    return hidden_grad, partial_value


def one_section(operands):
    grads, inputs, hidden, routes, weights_down, router = operands

    def per_expert(carry, expert_number):
        proj = jnp.dot(grads, weights_down[expert_number].T, preferred_element_type=jnp.float32).astype(jnp.bfloat16)
        carry = jnp.where((routes == expert_number)[:, :, None], proj[:, None, :], carry)
        return carry, None

    start = jnp.zeros((TOKENS, TOPK, HID), jnp.bfloat16)
    back, unused = lax.scan(per_expert, start, jnp.arange(EXPERTS, dtype=jnp.int32))
    return token_math(back, hidden, inputs, routes, router)


def reference(out_grad, saved_input, saved_hidden, expert_ids, down_weight, router_weight):
    count = N_PIPE * 2
    operands = (out_grad.reshape(count, TOKENS, DW), saved_input.reshape(count, TOKENS, DW),
                saved_hidden.reshape(count, TOKENS, TOPK, HID), expert_ids.reshape(count, TOKENS, TOPK),
                down_weight.reshape(count, EXPERTS, HID, DW), router_weight.reshape(count, EXPERTS, DW))
    hidden_grad, partial_value = lax.map(one_section, operands)
    partial_value = partial_value.reshape(N_PIPE, 2, EXPERTS, DW)
    router_grad = partial_value + partial_value[::-1, ::-1]
    return hidden_grad.reshape(N_PIPE, 2, TOKENS, TOPK, HID), router_grad
```

```python
import functools

import jax
import jax.numpy as jnp
from jax import lax
from jax.experimental import pallas as pl
from jax.experimental.pallas import tpu as pltpu
from jax.sharding import PartitionSpec as P

ROUTE_SCALE = 2.5
NX, NY, NC = 4, 2, 2
N_PIPE = 8
EXPERTS = NX * NY * NC
MIB = 1024 * 1024


def expert_at(x, y, c):
    return ((x % NX) * NY + y % NY) * NC + c % NC


def shift(dx, dy, dc):
    return [
        (expert_at(x, y, c), expert_at(x + dx, y + dy, c + dc))
        for x in range(NX)
        for y in range(NY)
        for c in range(NC)
    ]


def send(block, dx, dy, dc):
    return lax.ppermute(block, "expert", shift(dx, dy, dc))


def send_mirror(block, dy, dc):
    route = [
        (p * EXPERTS + low, (N_PIPE - 1 - p) * EXPERTS + high)
        for p in range(N_PIPE)
        for low, high in shift(0, dy, dc)
    ]
    return lax.ppermute(block, ("pipe", "expert"), route)


def project_kernel(n, *refs):
    blocks, weight, outs = refs[:n], refs[n], refs[n + 1 :]
    slot, tile = pl.program_id(0), pl.program_id(1)
    tok = blocks[0].shape[0] // 2
    wide = weight.shape[2]
    rows = pl.ds(pl.multiple_of(slot * tok, tok), tok)
    cols = pl.ds(pl.multiple_of(tile * wide, wide), wide)
    tokens = jnp.concatenate([b[rows, :] for b in blocks], axis=0)
    made = lax.dot_general(
        tokens, weight[0, 0], (((1,), (1,)), ((), ())), preferred_element_type=jnp.float32
    ).astype(jnp.bfloat16)
    for i, out in enumerate(outs):
        out[rows, cols] = made[i * tok : (i + 1) * tok]


def project(blocks, weight):
    n = len(blocks)
    rows, depth = blocks[0].shape
    hid = weight.shape[1]
    wide = 512
    whole = pl.BlockSpec((rows, depth), lambda s, h: (0, 0))
    return pl.pallas_call(
        functools.partial(project_kernel, n),
        grid=(2, hid // wide),
        in_specs=[whole] * n
        + [pl.BlockSpec((1, 1, wide, depth), lambda s, h: (s, 0, h, 0))],
        out_specs=[pl.BlockSpec((rows, hid), lambda s, h: (0, 0))] * n,
        out_shape=[jax.ShapeDtypeStruct((rows, hid), jnp.bfloat16)] * n,
        compiler_params=pltpu.CompilerParams(vmem_limit_bytes=36 * MIB),
        cost_estimate=pl.CostEstimate(
            flops=2 * n * rows * depth * hid,
            bytes_accessed=2 * (2 * hid * depth + n * rows * (depth + hid)),
            transcendentals=0,
        ),
    )(*blocks, weight[:, None])


def token_kernel(source, ids, probs, inputs, hidden, *refs):
    returned, (grad, part, held) = refs[:EXPERTS], refs[EXPERTS:]
    slot, group = pl.program_id(0), pl.program_id(1)
    tok, top = 16, 8
    first = pl.multiple_of((slot * pl.num_programs(1) + group) * tok, tok)
    rows = jnp.concatenate([r[pl.ds(first, tok), :] for r in returned], axis=0)
    routes = ids[...]
    shape = (tok * top, EXPERTS * tok)
    mine = lax.broadcasted_iota(jnp.int32, shape, 0) // top == lax.broadcasted_iota(
        jnp.int32, shape, 1
    ) % tok
    pick = jnp.where(jnp.logical_and(mine, routes == source[...]), 1.0, 0.0).astype(jnp.bfloat16)
    back = jnp.dot(pick, rows, preferred_element_type=jnp.float32)
    dgate = jnp.sum(hidden[...].astype(jnp.float32) * back, axis=1, keepdims=True)
    dgate = dgate.reshape(tok, top, 1)
    member = routes.reshape(tok, top, 1) == lax.broadcasted_iota(
        jnp.int32, (tok, top, EXPERTS), 2
    )
    chosen = jnp.sum(jnp.where(member, probs[...][:, None, :], 0.0), axis=2, keepdims=True)
    total = jnp.sum(chosen, axis=1, keepdims=True)
    share = chosen / total
    grad[...] = ((ROUTE_SCALE * share).reshape(tok * top, 1) * back).astype(jnp.bfloat16)
    centred = dgate - jnp.sum(share * dgate, axis=1, keepdims=True)
    selected = ROUTE_SCALE / total * centred * chosen * (1.0 - chosen)
    held[pl.ds(pl.multiple_of(group * tok, tok), tok), :] = jnp.sum(
        jnp.where(member, selected, 0.0), axis=1
    )

    @pl.when(group == pl.num_programs(1) - 1)
    def _():
        logit = held[...]
        high = logit.astype(jnp.bfloat16)
        low = (logit - high.astype(jnp.float32)).astype(jnp.bfloat16)
        over = (((0,), (0,)), ((), ()))
        values = inputs[...]
        made = lax.dot_general(high, values, over, preferred_element_type=jnp.float32)
        made += lax.dot_general(low, values, over, preferred_element_type=jnp.float32)
        part[0] = made.astype(jnp.bfloat16)


def token_math(source, ids, probs, inputs, hidden, returned):
    rows, depth = inputs.shape
    tok, top, hid = 16, 8, hidden.shape[1]
    slot_rows = rows // 2
    groups = slot_rows // tok
    step = lambda s, g: (s * groups + g, 0)
    fixed = lambda s, g: (0, 0)
    return pl.pallas_call(
        token_kernel,
        grid=(2, groups),
        in_specs=[
            pl.BlockSpec((1, EXPERTS * tok), fixed),
            pl.BlockSpec((tok * top, 1), step),
            pl.BlockSpec((tok, EXPERTS), step),
            pl.BlockSpec((slot_rows, depth), lambda s, g: (s, 0)),
            pl.BlockSpec((tok * top, hid), step),
        ]
        + [pl.BlockSpec((rows, hid), fixed)] * EXPERTS,
        out_specs=[
            pl.BlockSpec((tok * top, hid), step),
            pl.BlockSpec((1, EXPERTS, depth), lambda s, g: (s, 0, 0)),
        ],
        out_shape=[
            jax.ShapeDtypeStruct((rows * top, hid), jnp.bfloat16),
            jax.ShapeDtypeStruct((2, EXPERTS, depth), jnp.bfloat16),
        ],
        scratch_shapes=[pltpu.VMEM((slot_rows, EXPERTS), jnp.float32)],
        compiler_params=pltpu.CompilerParams(vmem_limit_bytes=32 * MIB),
        cost_estimate=pl.CostEstimate(
            flops=2 * rows * top * hid * EXPERTS * tok,
            bytes_accessed=2 * rows * hid * (2 * top + EXPERTS),
            transcendentals=0,
        ),
    )(source, ids, probs, inputs, hidden, *returned)


def gather(own):
    across = send(own, 0, 1, 0)
    from_low = send(own, 1, 0, 0)
    from_high = send(own, -1, 0, 0)
    from_low_across = send(across, 1, 0, 0)
    from_high_across = send(across, -1, 0, 0)
    far = send(from_low, 1, 0, 0)
    far_across = send(from_high_across, -1, 0, 0)
    return {
        0: (own, across),
        -1: (from_low, from_low_across),
        1: (from_high, from_high_across),
        2: (far, far_across),
    }


def reduce_router(part, core):
    wide = jnp.float32
    narrow = jnp.bfloat16
    first = core == 0
    keep = jnp.where(first, part[0], part[1])
    give = jnp.where(first, part[1], part[0])
    pair = (keep.astype(wide) + send(give, 0, 0, 1).astype(wide)).astype(narrow)
    low, high, far = send(pair, 1, 0, 0), send(pair, -1, 0, 0), send(pair, 2, 0, 0)
    line = (
        (pair.astype(wide) + far.astype(wide)) + (low.astype(wide) + high.astype(wide))
    ).astype(narrow)
    other = send(line, 0, 1, 0)
    mirror, mirror_other = send_mirror(line, 0, 1), send_mirror(line, 1, 1)
    total = (line.astype(wide) + other.astype(wide)) + (
        mirror.astype(wide) + mirror_other.astype(wide)
    )
    sibling = send(total, 0, 0, 1)
    return jnp.stack([jnp.where(first, total, sibling), jnp.where(first, sibling, total)])


def local(out_grad, saved_input, saved_hidden, expert_ids, down_weight, router_weight):
    tok, depth = out_grad.shape[2:]
    top, hid = saved_hidden.shape[3:]
    rows = 2 * tok
    me = lax.axis_index("expert")
    x, y, c = me // (NY * NC), me // NC % NY, me % NC

    logits = jnp.einsum(
        "std,sed->ste", saved_input[0], router_weight[0], preferred_element_type=jnp.float32
    )
    probs = jax.nn.sigmoid(logits).reshape(rows, EXPERTS)
    ids = expert_ids.reshape(rows * top, 1)

    own = out_grad.reshape(rows, depth)
    weight = down_weight.reshape(2, hid, depth)
    returned, source = [], []
    for dx, (near, across) in gather(own).items():
        blocks = [near, across, send(near, 0, 0, 1), send(across, 0, 0, 1)]
        projected = project(blocks, weight)
        for i, made in enumerate(projected):
            dy, dc = i % 2, i // 2
            away = (dx, dy, dc)
            returned.append(send(made, *away) if any(away) else made)
            source.append(expert_at(x - dx, y + dy, c + dc))
    marks = jnp.repeat(jnp.stack(source).astype(jnp.int32), 16)[None]
    grad, part = token_math(
        marks, ids, probs, saved_input.reshape(rows, depth), saved_hidden.reshape(rows * top, hid), returned
    )
    return grad.reshape(saved_hidden.shape), reduce_router(part, c)[None]


def solution(mesh):
    in_specs = (
        P("pipe", None, "expert", None),
        P("pipe", None, "expert", None),
        P("pipe", None, "expert", None, None),
        P("pipe", None, "expert", None),
        P("pipe", None, "expert", None, None),
        P("pipe", None, None, None),
    )
    out_specs = (P("pipe", None, "expert", None, None), P("pipe", None, None, None))
    return jax.shard_map(local, mesh=mesh, in_specs=in_specs, out_specs=out_specs, check_vma=False)
```

```python
import functools

import jax
import jax.numpy as jnp
import numpy as np
from jax import lax
from jax.experimental import pallas as pl
from jax.experimental.pallas import tpu as pltpu
from jax.sharding import PartitionSpec as P

ROUTE_SCALE = 2.5
NX, NY, NC = 4, 2, 2
N_PIPE = 8
CUTS = 2
EXPERTS = NX * NY * NC
MIB = 1024 * 1024


def expert_at(x, y, c):
    return ((x % NX) * NY + y % NY) * NC + c % NC


def shift(dx, dy, dc):
    return [
        (expert_at(x, y, c), expert_at(x + dx, y + dy, c + dc))
        for x in range(NX)
        for y in range(NY)
        for c in range(NC)
    ]


def send(block, dx, dy, dc):
    return lax.ppermute(block, "expert", shift(dx, dy, dc))


def after(block, *earlier):
    return lax.optimization_barrier((block, *earlier))[0]


def send_mirror(block, dy, dc):
    route = [
        (p * EXPERTS + low, (N_PIPE - 1 - p) * EXPERTS + high)
        for p in range(N_PIPE)
        for low, high in shift(0, dy, dc)
    ]
    return lax.ppermute(block, ("pipe", "expert"), route)


def project_kernel(layout, depth_of, *refs):
    n, n_in = len(layout), sum(len(group) for group in layout)
    blocks, weights, outs = refs[:n_in], refs[n_in : n_in + NC], refs[n_in + NC : n_in + NC + n]
    tokens, held, stage, token_sem, weight_sem, out_sem = refs[n_in + NC + n :]
    tok = tokens.shape[0] // (2 * n)
    wide = held.shape[2]
    tiles = weights[0].shape[1] // wide

    def token_copy(slot, i):
        group = layout[i]
        if len(group) == 1:
            source = blocks[group[0]].at[pl.ds(slot * tok, tok)]
        else:
            source = blocks[group[slot]]
        target = tokens.at[pl.ds((slot * n + i) * tok, tok)]
        return pltpu.make_async_copy(source, target, token_sem.at[slot, i])

    def weight_copy(step, e):
        place = lax.rem(step, depth_of)
        return pltpu.make_async_copy(
            weights[e].at[step // tiles, pl.ds(lax.rem(step, tiles) * wide, wide)],
            held.at[place, e],
            weight_sem.at[place, e],
        )

    def out_copy(slot, i):
        return pltpu.make_async_copy(
            stage.at[slot, i], outs[i].at[:, pl.ds(slot * tok, tok)], out_sem.at[slot, i]
        )

    for i in range(n):
        token_copy(0, i).start()
    for e in range(NC):
        weight_copy(0, e).start()
    for i in range(n):
        token_copy(1, i).start()
    for step in range(1, depth_of):
        for e in range(NC):
            weight_copy(step, e).start()

    def body(step, carry):
        slot, tile = step // tiles, lax.rem(step, tiles)
        for s in range(2):

            @pl.when(step == s * tiles)
            def _(s=s):
                for i in range(n):
                    token_copy(s, i).wait()

        rows = pl.ds(pl.multiple_of(slot * n * tok, tok), n * tok)
        cols = pl.ds(pl.multiple_of(tile * wide, wide), wide)
        for e in range(NC):
            weight_copy(step, e).wait()
            made = lax.dot_general(
                tokens[rows, :],
                held[lax.rem(step, depth_of), e],
                (((1,), (1,)), ((), ())),
                preferred_element_type=jnp.float32,
            ).astype(jnp.bfloat16)
            for i in range(n):
                stage[slot, i, e, :, cols] = made[i * tok : (i + 1) * tok]

            @pl.when(step + depth_of < 2 * tiles)
            def _(e=e):
                weight_copy(step + depth_of, e).start()

        for s in range(2):

            @pl.when(step == (s + 1) * tiles - 1)
            def _(s=s):
                for i in range(n):
                    out_copy(s, i).start()

        return carry

    lax.fori_loop(0, 2 * tiles, body, 0)
    for s in range(2):
        for i in range(n):
            out_copy(s, i).wait()


def project(shards, own, sibling):
    layout, blocks = [], []
    for shard in shards:
        shard = shard if isinstance(shard, tuple) else (shard,)
        layout.append(tuple(range(len(blocks), len(blocks) + len(shard))))
        blocks += shard
    n = len(shards)
    _, hid, depth = own.shape
    tok = blocks[0].shape[0] // 2
    wide, depth_of = 512, 2
    anywhere = pl.BlockSpec(memory_space=pl.ANY)
    return pl.pallas_call(
        functools.partial(project_kernel, layout, depth_of),
        in_specs=[anywhere] * (len(blocks) + NC),
        out_specs=[anywhere] * n,
        out_shape=[jax.ShapeDtypeStruct((NC, 2 * tok, hid), jnp.bfloat16)] * n,
        scratch_shapes=[
            pltpu.VMEM((2 * n * tok, depth), jnp.bfloat16),
            pltpu.VMEM((depth_of, NC, wide, depth), jnp.bfloat16),
            pltpu.VMEM((2, n, NC, tok, hid), jnp.bfloat16),
            pltpu.SemaphoreType.DMA((2, n)),
            pltpu.SemaphoreType.DMA((depth_of, NC)),
            pltpu.SemaphoreType.DMA((2, n)),
        ],
        compiler_params=pltpu.CompilerParams(vmem_limit_bytes=48 * MIB),
        cost_estimate=pl.CostEstimate(
            flops=8 * n * tok * depth * hid,
            bytes_accessed=8 * hid * depth + 4 * n * tok * (depth + 2 * hid),
            transcendentals=0,
        ),
    )(*blocks, own, sibling)


def token_kernel(n, source, ids, probs, inputs, hidden, *refs):
    returned, (grad, part) = refs[:n], refs[n : n + 2]
    rows_in, hidden_in, inputs_in, grad_out, logits, row_sem, sems, out_sem = refs[n + 2 :]
    chunks, tok, top = hidden_in.shape[0], 16, 8
    span = rows_in.shape[1] // chunks
    half = rows_in.shape[1] // 2

    def row_copy(q, i):
        place = pl.ds(q * span, span)
        return pltpu.make_async_copy(
            returned[i].at[:, place], rows_in.at[pl.ds(NC * i, NC), place], row_sem.at[q, i]
        )

    def hidden_copy(q):
        source = hidden.at[pl.ds(q * span * top, span * top)]
        return pltpu.make_async_copy(source, hidden_in.at[q], sems.at[q])

    def out_copy(q):
        target = grad.at[pl.ds(q * span * top, span * top)]
        return pltpu.make_async_copy(grad_out.at[q], target, out_sem.at[q])

    inputs_copy = pltpu.make_async_copy(inputs, inputs_in, sems.at[chunks])
    for q in range(chunks):
        for i in range(n):
            row_copy(q, i).start()
        hidden_copy(q).start()
    inputs_copy.start()

    shape = (tok * top, EXPERTS * tok)
    mine = lax.broadcasted_iota(jnp.int32, shape, 0) // top == lax.broadcasted_iota(
        jnp.int32, shape, 1
    ) % tok
    for q in range(chunks):
        for i in range(n):
            row_copy(q, i).wait()
        hidden_copy(q).wait()
        for g in range(span // tok):
            first = q * span + g * tok
            at = slice(g * tok * top, (g + 1) * tok * top)
            rows = jnp.concatenate(
                [rows_in[e, first : first + tok, :] for e in range(EXPERTS)], axis=0
            )
            routes = ids[first * top : (first + tok) * top, :]
            pick = jnp.where(jnp.logical_and(mine, routes == source[...]), 1.0, 0.0)
            back = jnp.dot(pick.astype(jnp.bfloat16), rows, preferred_element_type=jnp.float32)
            dgate = jnp.sum(hidden_in[q, at, :].astype(jnp.float32) * back, axis=1, keepdims=True)
            dgate = dgate.reshape(tok, top, 1)
            member = routes.reshape(tok, top, 1) == lax.broadcasted_iota(
                jnp.int32, (tok, top, EXPERTS), 2
            )
            chosen = jnp.sum(
                jnp.where(member, probs[first : first + tok, :][:, None, :], 0.0),
                axis=2,
                keepdims=True,
            )
            total = jnp.sum(chosen, axis=1, keepdims=True)
            share = chosen / total
            weights = (ROUTE_SCALE * share).reshape(tok * top, 1)
            grad_out[q, at, :] = (weights * back).astype(jnp.bfloat16)
            centred = dgate - jnp.sum(share * dgate, axis=1, keepdims=True)
            selected = ROUTE_SCALE / total * centred * chosen * (1.0 - chosen)
            logits[first : first + tok, :] = jnp.sum(jnp.where(member, selected, 0.0), axis=1)
        out_copy(q).start()

    inputs_copy.wait()
    for s in range(2):
        logit = logits[s * half : (s + 1) * half, :]
        high = logit.astype(jnp.bfloat16)
        low = (logit - high.astype(jnp.float32)).astype(jnp.bfloat16)
        over = (((0,), (0,)), ((), ()))
        values = inputs_in[s * half : (s + 1) * half, :]
        made = lax.dot_general(high, values, over, preferred_element_type=jnp.float32)
        part[s] = made + lax.dot_general(low, values, over, preferred_element_type=jnp.float32)
    for q in range(chunks):
        out_copy(q).wait()


def token_math(source, ids, probs, inputs, hidden, returned):
    rows, depth = inputs.shape
    top, hid = 8, hidden.shape[1]
    n, chunks = len(returned), 4
    span = rows // chunks
    inside = pl.BlockSpec(memory_space=pltpu.VMEM)
    anywhere = pl.BlockSpec(memory_space=pl.ANY)
    return pl.pallas_call(
        functools.partial(token_kernel, n),
        in_specs=[inside] * 3 + [anywhere] * (2 + n),
        out_specs=[anywhere, inside],
        out_shape=[
            jax.ShapeDtypeStruct((rows * top, hid), jnp.bfloat16),
            jax.ShapeDtypeStruct((2, EXPERTS, depth), jnp.float32),
        ],
        scratch_shapes=[
            pltpu.VMEM((EXPERTS, rows, hid), jnp.bfloat16),
            pltpu.VMEM((chunks, span * top, hid), jnp.bfloat16),
            pltpu.VMEM((rows, depth), jnp.bfloat16),
            pltpu.VMEM((chunks, span * top, hid), jnp.bfloat16),
            pltpu.VMEM((rows, EXPERTS), jnp.float32),
            pltpu.SemaphoreType.DMA((chunks, n)),
            pltpu.SemaphoreType.DMA((chunks + 1,)),
            pltpu.SemaphoreType.DMA((chunks,)),
        ],
        compiler_params=pltpu.CompilerParams(vmem_limit_bytes=32 * MIB),
        cost_estimate=pl.CostEstimate(
            flops=2 * rows * top * hid * EXPERTS * 16,
            bytes_accessed=2 * rows * hid * (2 * top + EXPERTS),
            transcendentals=0,
        ),
    )(source, ids, probs, inputs, hidden, *returned)


def reduce_router(part, core):
    wide = jnp.float32
    narrow = jnp.bfloat16
    first = core == 0
    keep = jnp.where(first, part[0], part[1])
    give = jnp.where(first, part[1], part[0])
    pair = (keep + send(give, 0, 0, 1)).astype(narrow)
    low, high, far = send(pair, 1, 0, 0), send(pair, -1, 0, 0), send(pair, 2, 0, 0)
    line = (
        (pair.astype(wide) + far.astype(wide)) + (low.astype(wide) + high.astype(wide))
    ).astype(narrow)
    other = send(line, 0, 1, 0)
    mirror, mirror_other = send_mirror(line, 0, 1), send_mirror(line, 1, 1)
    total = (line.astype(wide) + other.astype(wide)) + (
        mirror.astype(wide) + mirror_other.astype(wide)
    )
    sibling = send(total, 0, 0, 1)
    return jnp.stack([jnp.where(first, total, sibling), jnp.where(first, sibling, total)])


def local(out_grad, saved_input, saved_hidden, expert_ids, down_weight, router_weight):
    tok, depth = out_grad.shape[2:]
    top, hid = saved_hidden.shape[3:]
    rows = 2 * tok
    me = lax.axis_index("expert")

    logits = jnp.einsum(
        "std,sed->ste", saved_input[0], router_weight[0], preferred_element_type=jnp.float32
    )
    probs = jax.nn.sigmoid(logits).reshape(rows, EXPERTS)
    ids = expert_ids.reshape(rows * top, 1)

    own = out_grad.reshape(rows, depth)
    weight = down_weight.reshape(2, hid, depth)

    across = send(own, 0, 1, 0)
    sibling_weight = send(weight, 0, 0, 1)
    first, second = out_grad[0, 0], out_grad[0, 1]
    low, high = [send(first, 1, 0, 0)], [send(second, -1, 0, 0)]
    far = send(low[0], 1, 0, 0), send(high[0], -1, 0, 0)
    low, high = (low[0], send(second, 1, 0, 0)), (send(first, -1, 0, 0), high[0])
    far_across = send(far[0], 0, 1, 0), send(far[1], 0, 1, 0)
    low_across, high_across = send(across, 1, 0, 0), send(across, -1, 0, 0)
    early = project([own, across, low, high, far], weight, sibling_weight)
    low_across = after(low_across, early[0])
    late = project([low_across, high_across, far_across], weight, sibling_weight)
    places = [(0, 0), (0, 1), (-1, 0), (1, 0), (2, 0), (-1, 1), (1, 1), (2, 1)]
    returned = []
    for i, ((dx, dy), made) in enumerate(zip(places, early + late)):
        if i >= len(early):
            made = after(made, returned[1])
        returned.append(send(made, dx, dy, 0) if dx or dy else made)
    table = np.array(
        [
            [
                expert_at(me // (NY * NC) - dx, me // NC % NY + dy, me % NC + dc)
                for dx, dy in places
                for dc in range(NC)
                for _ in range(16)
            ]
            for me in range(EXPERTS)
        ],
        np.int32,
    )
    marks = lax.dynamic_slice_in_dim(jnp.asarray(table), me, 1, 0)
    grad, part = token_math(
        marks, ids, probs, saved_input.reshape(rows, depth), saved_hidden.reshape(rows * top, hid), returned
    )
    return grad.reshape(saved_hidden.shape), reduce_router(part, lax.rem(me, NC))[None]


def solution(mesh):
    in_specs = (
        P("pipe", None, "expert", None),
        P("pipe", None, "expert", None),
        P("pipe", None, "expert", None, None),
        P("pipe", None, "expert", None),
        P("pipe", None, "expert", None, None),
        P("pipe", None, None, None),
    )
    out_specs = (P("pipe", None, "expert", None, None), P("pipe", None, None, None))
    return jax.shard_map(local, mesh=mesh, in_specs=in_specs, out_specs=out_specs, check_vma=False)
```

```python
import functools

import jax
import jax.numpy as jnp
import numpy as np
from jax import lax
from jax.experimental import pallas as pl
from jax.experimental.pallas import tpu as pltpu
from jax.sharding import PartitionSpec as P

ROUTE_SCALE = 2.5
NX, NY, NC = 4, 2, 2
N_PIPE = 8
CUTS = 2
EXPERTS = NX * NY * NC
MIB = 1024 * 1024


def expert_at(x, y, c):
    return ((x % NX) * NY + y % NY) * NC + c % NC


def shift(dx, dy, dc):
    return [
        (expert_at(x, y, c), expert_at(x + dx, y + dy, c + dc))
        for x in range(NX)
        for y in range(NY)
        for c in range(NC)
    ]


def send(block, dx, dy, dc):
    return lax.ppermute(block, "expert", shift(dx, dy, dc))


def after(block, *earlier):
    return lax.optimization_barrier((block, *earlier))[0]


def send_mirror(block, dy, dc):
    route = [
        (p * EXPERTS + low, (N_PIPE - 1 - p) * EXPERTS + high)
        for p in range(N_PIPE)
        for low, high in shift(0, dy, dc)
    ]
    return lax.ppermute(block, ("pipe", "expert"), route)


def project_kernel(layout, depth_of, *refs):
    n, n_in = len(layout), sum(len(group) for group in layout)
    blocks, weights, outs = refs[:n_in], refs[n_in : n_in + NC], refs[n_in + NC : n_in + NC + n]
    tokens, held, stage, token_sem, weight_sem, out_sem = refs[n_in + NC + n :]
    tok = tokens.shape[0] // (2 * n)
    wide = held.shape[2]
    tiles = weights[0].shape[1] // wide

    def token_copy(slot, i):
        group = layout[i]
        if len(group) == 1:
            source = blocks[group[0]].at[pl.ds(slot * tok, tok)]
        else:
            source = blocks[group[slot]]
        target = tokens.at[pl.ds((slot * n + i) * tok, tok)]
        return pltpu.make_async_copy(source, target, token_sem.at[slot, i])

    def weight_copy(step, e):
        place = lax.rem(step, depth_of)
        return pltpu.make_async_copy(
            weights[e].at[step // tiles, pl.ds(lax.rem(step, tiles) * wide, wide)],
            held.at[place, e],
            weight_sem.at[place, e],
        )

    def out_copy(slot, i):
        return pltpu.make_async_copy(
            stage.at[slot, i], outs[i].at[:, pl.ds(slot * tok, tok)], out_sem.at[slot, i]
        )

    for i in range(n):
        token_copy(0, i).start()
    for e in range(NC):
        weight_copy(0, e).start()
    for i in range(n):
        token_copy(1, i).start()
    for step in range(1, depth_of):
        for e in range(NC):
            weight_copy(step, e).start()

    def body(step, carry):
        slot, tile = step // tiles, lax.rem(step, tiles)
        for s in range(2):

            @pl.when(step == s * tiles)
            def _(s=s):
                for i in range(n):
                    token_copy(s, i).wait()

        rows = pl.ds(pl.multiple_of(slot * n * tok, tok), n * tok)
        cols = pl.ds(pl.multiple_of(tile * wide, wide), wide)
        for e in range(NC):
            weight_copy(step, e).wait()
            made = lax.dot_general(
                tokens[rows, :],
                held[lax.rem(step, depth_of), e],
                (((1,), (1,)), ((), ())),
                preferred_element_type=jnp.float32,
            ).astype(jnp.bfloat16)
            for i in range(n):
                stage[slot, i, e, :, cols] = made[i * tok : (i + 1) * tok]

            @pl.when(step + depth_of < 2 * tiles)
            def _(e=e):
                weight_copy(step + depth_of, e).start()

        for s in range(2):

            @pl.when(step == (s + 1) * tiles - 1)
            def _(s=s):
                for i in range(n):
                    out_copy(s, i).start()

        return carry

    lax.fori_loop(0, 2 * tiles, body, 0)
    for s in range(2):
        for i in range(n):
            out_copy(s, i).wait()


def project(shards, own, sibling):
    layout, blocks = [], []
    for shard in shards:
        shard = shard if isinstance(shard, tuple) else (shard,)
        layout.append(tuple(range(len(blocks), len(blocks) + len(shard))))
        blocks += shard
    n = len(shards)
    _, hid, depth = own.shape
    tok = blocks[0].shape[0] // 2
    wide, depth_of = 512, 2
    anywhere = pl.BlockSpec(memory_space=pl.ANY)
    return pl.pallas_call(
        functools.partial(project_kernel, layout, depth_of),
        in_specs=[anywhere] * (len(blocks) + NC),
        out_specs=[anywhere] * n,
        out_shape=[jax.ShapeDtypeStruct((NC, 2 * tok, hid), jnp.bfloat16)] * n,
        scratch_shapes=[
            pltpu.VMEM((2 * n * tok, depth), jnp.bfloat16),
            pltpu.VMEM((depth_of, NC, wide, depth), jnp.bfloat16),
            pltpu.VMEM((2, n, NC, tok, hid), jnp.bfloat16),
            pltpu.SemaphoreType.DMA((2, n)),
            pltpu.SemaphoreType.DMA((depth_of, NC)),
            pltpu.SemaphoreType.DMA((2, n)),
        ],
        compiler_params=pltpu.CompilerParams(vmem_limit_bytes=48 * MIB),
        cost_estimate=pl.CostEstimate(
            flops=8 * n * tok * depth * hid,
            bytes_accessed=8 * hid * depth + 4 * n * tok * (depth + 2 * hid),
            transcendentals=0,
        ),
    )(*blocks, own, sibling)


def token_kernel(n, source, ids, probs, inputs, *refs):
    hidden, returned, (grad, part) = refs[:2], refs[2 : n + 2], refs[n + 2 : n + 4]
    grad_out, logits, out_sem = refs[n + 4 :]
    chunks, tok, top = grad_out.shape[0], 16, 8
    half = inputs.shape[0] // 2
    span = 2 * half // chunks

    def out_copy(q):
        target = grad.at[pl.ds(q * span * top, span * top)]
        return pltpu.make_async_copy(grad_out.at[q], target, out_sem.at[q])

    shape = (tok * top, EXPERTS * tok)
    mine = lax.broadcasted_iota(jnp.int32, shape, 0) // top == lax.broadcasted_iota(
        jnp.int32, shape, 1
    ) % tok
    for q in range(chunks):
        for g in range(span // tok):
            first = q * span + g * tok
            at = slice(g * tok * top, (g + 1) * tok * top)
            slot, within = first // half, first % half * top
            rows = jnp.concatenate(
                [r[e, first : first + tok, :] for r in returned for e in range(NC)], axis=0
            )
            routes = ids[first * top : (first + tok) * top, :]
            pick = jnp.where(jnp.logical_and(mine, routes == source[...]), 1.0, 0.0)
            back = jnp.dot(pick.astype(jnp.bfloat16), rows, preferred_element_type=jnp.float32)
            saved = hidden[slot][within : within + tok * top, :].astype(jnp.float32)
            dgate = jnp.sum(saved * back, axis=1, keepdims=True).reshape(tok, top, 1)
            member = routes.reshape(tok, top, 1) == lax.broadcasted_iota(
                jnp.int32, (tok, top, EXPERTS), 2
            )
            chosen = jnp.sum(
                jnp.where(member, probs[first : first + tok, :][:, None, :], 0.0),
                axis=2,
                keepdims=True,
            )
            total = jnp.sum(chosen, axis=1, keepdims=True)
            share = chosen / total
            weights = (ROUTE_SCALE * share).reshape(tok * top, 1)
            grad_out[q, at, :] = (weights * back).astype(jnp.bfloat16)
            centred = dgate - jnp.sum(share * dgate, axis=1, keepdims=True)
            selected = ROUTE_SCALE / total * centred * chosen * (1.0 - chosen)
            logits[first : first + tok, :] = jnp.sum(jnp.where(member, selected, 0.0), axis=1)
        out_copy(q).start()

    for s in range(2):
        logit = logits[s * half : (s + 1) * half, :]
        high = logit.astype(jnp.bfloat16)
        low = (logit - high.astype(jnp.float32)).astype(jnp.bfloat16)
        over = (((0,), (0,)), ((), ()))
        values = inputs[s * half : (s + 1) * half, :]
        made = lax.dot_general(high, values, over, preferred_element_type=jnp.float32)
        part[s] = made + lax.dot_general(low, values, over, preferred_element_type=jnp.float32)
    for q in range(chunks):
        out_copy(q).wait()


def token_math(source, ids, probs, inputs, hidden, returned):
    rows, depth = inputs.shape
    top, hid = 8, hidden[0].shape[1]
    n, chunks = len(returned), 4
    span = rows // chunks
    inside = pl.BlockSpec(memory_space=pltpu.VMEM)
    anywhere = pl.BlockSpec(memory_space=pl.ANY)
    return pl.pallas_call(
        functools.partial(token_kernel, n),
        in_specs=[inside] * (6 + n),
        out_specs=[anywhere, inside],
        out_shape=[
            jax.ShapeDtypeStruct((rows * top, hid), jnp.bfloat16),
            jax.ShapeDtypeStruct((2, EXPERTS, depth), jnp.float32),
        ],
        scratch_shapes=[
            pltpu.VMEM((chunks, span * top, hid), jnp.bfloat16),
            pltpu.VMEM((rows, EXPERTS), jnp.float32),
            pltpu.SemaphoreType.DMA((chunks,)),
        ],
        compiler_params=pltpu.CompilerParams(vmem_limit_bytes=16 * MIB),
        cost_estimate=pl.CostEstimate(
            flops=2 * rows * top * hid * EXPERTS * 16,
            bytes_accessed=2 * rows * hid * (2 * top + EXPERTS),
            transcendentals=0,
        ),
    )(source, ids, probs, inputs, *hidden, *returned)


def reduce_router(part, core):
    wide = jnp.float32
    narrow = jnp.bfloat16
    first = core == 0
    keep = jnp.where(first, part[0], part[1])
    give = jnp.where(first, part[1], part[0])
    pair = (keep + send(give, 0, 0, 1)).astype(narrow)
    low, high, far = send(pair, 1, 0, 0), send(pair, -1, 0, 0), send(pair, 2, 0, 0)
    line = (
        (pair.astype(wide) + far.astype(wide)) + (low.astype(wide) + high.astype(wide))
    ).astype(narrow)
    other = send(line, 0, 1, 0)
    mirror, mirror_other = send_mirror(line, 0, 1), send_mirror(line, 1, 1)
    total = (line.astype(wide) + other.astype(wide)) + (
        mirror.astype(wide) + mirror_other.astype(wide)
    )
    sibling = send(total, 0, 0, 1)
    return jnp.stack([jnp.where(first, total, sibling), jnp.where(first, sibling, total)])


def local(out_grad, saved_input, saved_hidden, expert_ids, down_weight, router_weight):
    tok, depth = out_grad.shape[2:]
    top, hid = saved_hidden.shape[3:]
    rows = 2 * tok
    me = lax.axis_index("expert")

    logits = jnp.einsum(
        "std,sed->ste", saved_input[0], router_weight[0], preferred_element_type=jnp.float32
    )
    probs = jax.nn.sigmoid(logits).reshape(rows, EXPERTS)
    ids = expert_ids.reshape(rows * top, 1)

    own = out_grad.reshape(rows, depth)
    weight = down_weight.reshape(2, hid, depth)

    across = send(own, 0, 1, 0)
    sibling_weight = send(weight, 0, 0, 1)
    first, second = out_grad[0, 0], out_grad[0, 1]
    low, high = [send(first, 1, 0, 0)], [send(second, -1, 0, 0)]
    far = send(low[0], 1, 0, 0), send(high[0], -1, 0, 0)
    low, high = (low[0], send(second, 1, 0, 0)), (send(first, -1, 0, 0), high[0])
    far_across = send(far[0], 0, 1, 0), send(far[1], 0, 1, 0)
    low_across, high_across = send(across, 1, 0, 0), send(across, -1, 0, 0)
    early = project([own, across, low, high, far], weight, sibling_weight)
    low_across = after(low_across, early[0])
    late = project([low_across, high_across, far_across], weight, sibling_weight)
    places = [(0, 0), (0, 1), (-1, 0), (1, 0), (2, 0), (-1, 1), (1, 1), (2, 1)]
    returned = []
    for i, ((dx, dy), made) in enumerate(zip(places, early + late)):
        if i >= len(early):
            made = after(made, returned[1])
        returned.append(send(made, dx, dy, 0) if dx or dy else made)
    table = np.array(
        [
            [
                expert_at(me // (NY * NC) - dx, me // NC % NY + dy, me % NC + dc)
                for dx, dy in places
                for dc in range(NC)
                for _ in range(16)
            ]
            for me in range(EXPERTS)
        ],
        np.int32,
    )
    marks = lax.dynamic_slice_in_dim(jnp.asarray(table), me, 1, 0)
    grad, part = token_math(
        marks, ids, probs, saved_input.reshape(rows, depth), [saved_hidden[0, s].reshape(tok * top, hid) for s in range(2)], returned
    )
    return grad.reshape(saved_hidden.shape), reduce_router(part, lax.rem(me, NC))[None]


def solution(mesh):
    in_specs = (
        P("pipe", None, "expert", None),
        P("pipe", None, "expert", None),
        P("pipe", None, "expert", None, None),
        P("pipe", None, "expert", None),
        P("pipe", None, "expert", None, None),
        P("pipe", None, None, None),
    )
    out_specs = (P("pipe", None, "expert", None, None), P("pipe", None, None, None))
    return jax.shard_map(local, mesh=mesh, in_specs=in_specs, out_specs=out_specs, check_vma=False)
```

```python
import functools

import jax
import jax.numpy as jnp
import numpy as np
from jax import lax
from jax.experimental import pallas as pl
from jax.experimental.pallas import tpu as pltpu
from jax.sharding import PartitionSpec as P

ROUTE_SCALE = 2.5
NX, NY, NC = 4, 2, 2
N_PIPE = 8
CUTS = 2
EXPERTS = NX * NY * NC
MIB = 1024 * 1024


def expert_at(x, y, c):
    return ((x % NX) * NY + y % NY) * NC + c % NC


def shift(dx, dy, dc):
    return [
        (expert_at(x, y, c), expert_at(x + dx, y + dy, c + dc))
        for x in range(NX)
        for y in range(NY)
        for c in range(NC)
    ]


def send(block, dx, dy, dc):
    return lax.ppermute(block, "expert", shift(dx, dy, dc))


def after(block, *earlier):
    return lax.optimization_barrier((block, *earlier))[0]


def send_mirror(block, dy, dc):
    route = [
        (p * EXPERTS + low, (N_PIPE - 1 - p) * EXPERTS + high)
        for p in range(N_PIPE)
        for low, high in shift(0, dy, dc)
    ]
    return lax.ppermute(block, ("pipe", "expert"), route)


def project_kernel(layout, depth_of, *refs):
    n, n_in = len(layout), sum(len(group) for group in layout)
    blocks, weights, outs = refs[:n_in], refs[n_in : n_in + NC], refs[n_in + NC : n_in + NC + n]
    tokens, held, stage, token_sem, weight_sem, out_sem = refs[n_in + NC + n :]
    tok = tokens.shape[0] // (2 * n)
    wide = held.shape[2]
    tiles = weights[0].shape[1] // wide

    def token_copy(slot, i):
        group = layout[i]
        if len(group) == 1:
            source = blocks[group[0]].at[pl.ds(slot * tok, tok)]
        else:
            source = blocks[group[slot]]
        target = tokens.at[pl.ds((slot * n + i) * tok, tok)]
        return pltpu.make_async_copy(source, target, token_sem.at[slot, i])

    def weight_copy(step, e):
        place = lax.rem(step, depth_of)
        return pltpu.make_async_copy(
            weights[e].at[step // tiles, pl.ds(lax.rem(step, tiles) * wide, wide)],
            held.at[place, e],
            weight_sem.at[place, e],
        )

    def out_copy(slot, i):
        return pltpu.make_async_copy(
            stage.at[slot, i], outs[i].at[:, pl.ds(slot * tok, tok)], out_sem.at[slot, i]
        )

    for i in range(n):
        token_copy(0, i).start()
    for e in range(NC):
        weight_copy(0, e).start()
    for i in range(n):
        token_copy(1, i).start()
    for step in range(1, depth_of):
        for e in range(NC):
            weight_copy(step, e).start()

    def body(step, carry):
        slot, tile = step // tiles, lax.rem(step, tiles)
        for s in range(2):

            @pl.when(step == s * tiles)
            def _(s=s):
                for i in range(n):
                    token_copy(s, i).wait()

        rows = pl.ds(pl.multiple_of(slot * n * tok, tok), n * tok)
        cols = pl.ds(pl.multiple_of(tile * wide, wide), wide)
        for e in range(NC):
            weight_copy(step, e).wait()
            made = lax.dot_general(
                tokens[rows, :],
                held[lax.rem(step, depth_of), e],
                (((1,), (1,)), ((), ())),
                preferred_element_type=jnp.float32,
            ).astype(jnp.bfloat16)
            for i in range(n):
                stage[slot, i, e, :, cols] = made[i * tok : (i + 1) * tok]

            @pl.when(step + depth_of < 2 * tiles)
            def _(e=e):
                weight_copy(step + depth_of, e).start()

        for s in range(2):

            @pl.when(step == (s + 1) * tiles - 1)
            def _(s=s):
                for i in range(n):
                    out_copy(s, i).start()

        return carry

    lax.fori_loop(0, 2 * tiles, body, 0)
    for s in range(2):
        for i in range(n):
            out_copy(s, i).wait()


def project(shards, own, sibling):
    layout, blocks = [], []
    for shard in shards:
        shard = shard if isinstance(shard, tuple) else (shard,)
        layout.append(tuple(range(len(blocks), len(blocks) + len(shard))))
        blocks += shard
    n = len(shards)
    _, hid, depth = own.shape
    tok = blocks[0].shape[0] // 2
    wide, depth_of = 512, 2
    anywhere = pl.BlockSpec(memory_space=pl.ANY)
    return pl.pallas_call(
        functools.partial(project_kernel, layout, depth_of),
        in_specs=[anywhere] * (len(blocks) + NC),
        out_specs=[anywhere] * n,
        out_shape=[jax.ShapeDtypeStruct((NC, 2 * tok, hid), jnp.bfloat16)] * n,
        scratch_shapes=[
            pltpu.VMEM((2 * n * tok, depth), jnp.bfloat16),
            pltpu.VMEM((depth_of, NC, wide, depth), jnp.bfloat16),
            pltpu.VMEM((2, n, NC, tok, hid), jnp.bfloat16),
            pltpu.SemaphoreType.DMA((2, n)),
            pltpu.SemaphoreType.DMA((depth_of, NC)),
            pltpu.SemaphoreType.DMA((2, n)),
        ],
        compiler_params=pltpu.CompilerParams(vmem_limit_bytes=48 * MIB),
        cost_estimate=pl.CostEstimate(
            flops=8 * n * tok * depth * hid,
            bytes_accessed=8 * hid * depth + 4 * n * tok * (depth + 2 * hid),
            transcendentals=0,
        ),
    )(*blocks, own, sibling)


def token_kernel(n, source, ids, probs, inputs, *refs):
    hidden, returned, (grad, part) = refs[:2], refs[2 : n + 2], refs[n + 2 : n + 4]
    grad_out, logits, out_sem = refs[n + 4 :]
    chunks, tok, top = grad_out.shape[0], 16, 8
    half = inputs.shape[0] // 2
    span = 2 * half // chunks

    def out_copy(q):
        target = grad.at[pl.ds(q * span * top, span * top)]
        return pltpu.make_async_copy(grad_out.at[q], target, out_sem.at[q])

    shape = (tok * top, EXPERTS * tok)
    mine = lax.broadcasted_iota(jnp.int32, shape, 0) // top == lax.broadcasted_iota(
        jnp.int32, shape, 1
    ) % tok
    for q in range(chunks):
        for g in range(span // tok):
            first = q * span + g * tok
            at = slice(g * tok * top, (g + 1) * tok * top)
            slot, within = first // half, first % half * top
            rows = jnp.concatenate(
                [r[e, first : first + tok, :] for r in returned for e in range(NC)], axis=0
            )
            routes = ids[first * top : (first + tok) * top, :]
            pick = jnp.where(jnp.logical_and(mine, routes == source[...]), 1.0, 0.0)
            back = jnp.dot(pick.astype(jnp.bfloat16), rows, preferred_element_type=jnp.float32)
            saved = hidden[slot][within : within + tok * top, :].astype(jnp.float32)
            dgate = jnp.sum(saved * back, axis=1, keepdims=True).reshape(tok, top, 1)
            member = routes.reshape(tok, top, 1) == lax.broadcasted_iota(
                jnp.int32, (tok, top, EXPERTS), 2
            )
            chosen = jnp.sum(
                jnp.where(member, probs[first : first + tok, :][:, None, :], 0.0),
                axis=2,
                keepdims=True,
            )
            total = jnp.sum(chosen, axis=1, keepdims=True)
            share = chosen / total
            weights = (ROUTE_SCALE * share).reshape(tok * top, 1)
            grad_out[q, at, :] = (weights * back).astype(jnp.bfloat16)
            centred = dgate - jnp.sum(share * dgate, axis=1, keepdims=True)
            selected = ROUTE_SCALE / total * centred * chosen * (1.0 - chosen)
            logits[first : first + tok, :] = jnp.sum(jnp.where(member, selected, 0.0), axis=1)
        out_copy(q).start()

    for s in range(2):
        logit = logits[s * half : (s + 1) * half, :]
        high = logit.astype(jnp.bfloat16)
        low = (logit - high.astype(jnp.float32)).astype(jnp.bfloat16)
        over = (((0,), (0,)), ((), ()))
        values = inputs[s * half : (s + 1) * half, :]
        made = lax.dot_general(high, values, over, preferred_element_type=jnp.float32)
        part[s] = made + lax.dot_general(low, values, over, preferred_element_type=jnp.float32)
    for q in range(chunks):
        out_copy(q).wait()


def token_math(source, ids, probs, inputs, hidden, returned):
    rows, depth = inputs.shape
    top, hid = 8, hidden[0].shape[1]
    n, chunks = len(returned), 4
    span = rows // chunks
    inside = pl.BlockSpec(memory_space=pltpu.VMEM)
    anywhere = pl.BlockSpec(memory_space=pl.ANY)
    return pl.pallas_call(
        functools.partial(token_kernel, n),
        in_specs=[inside] * (6 + n),
        out_specs=[anywhere, inside],
        out_shape=[
            jax.ShapeDtypeStruct((rows * top, hid), jnp.bfloat16),
            jax.ShapeDtypeStruct((2, EXPERTS, depth), jnp.float32),
        ],
        scratch_shapes=[
            pltpu.VMEM((chunks, span * top, hid), jnp.bfloat16),
            pltpu.VMEM((rows, EXPERTS), jnp.float32),
            pltpu.SemaphoreType.DMA((chunks,)),
        ],
        compiler_params=pltpu.CompilerParams(vmem_limit_bytes=16 * MIB),
        cost_estimate=pl.CostEstimate(
            flops=2 * rows * top * hid * EXPERTS * 16,
            bytes_accessed=2 * rows * hid * (2 * top + EXPERTS),
            transcendentals=0,
        ),
    )(source, ids, probs, inputs, *hidden, *returned)


def reduce_router(part, core):
    wide = jnp.float32
    narrow = jnp.bfloat16
    first = core == 0
    keep = jnp.where(first, part[0], part[1])
    give = jnp.where(first, part[1], part[0])
    pair = (keep + send(give, 0, 0, 1)).astype(narrow)
    low, high, far = send(pair, 1, 0, 0), send(pair, -1, 0, 0), send(pair, 2, 0, 0)
    line = (
        (pair.astype(wide) + far.astype(wide)) + (low.astype(wide) + high.astype(wide))
    ).astype(narrow)
    other = send(line, 0, 1, 0)
    mirror, mirror_other = send_mirror(line, 0, 1), send_mirror(line, 1, 1)
    total = (line.astype(wide) + other.astype(wide)) + (
        mirror.astype(wide) + mirror_other.astype(wide)
    )
    sibling = send(total, 0, 0, 1)
    here = jnp.arange(2)[:, None, None] == core
    return jnp.where(here, total[None], sibling[None])


def local(out_grad, saved_input, saved_hidden, expert_ids, down_weight, router_weight):
    tok, depth = out_grad.shape[2:]
    top, hid = saved_hidden.shape[3:]
    rows = 2 * tok
    me = lax.axis_index("expert")

    logits = jnp.einsum(
        "std,sed->ste", saved_input[0], router_weight[0], preferred_element_type=jnp.float32
    )
    probs = jax.nn.sigmoid(logits).reshape(rows, EXPERTS)
    ids = expert_ids.reshape(rows * top, 1)

    own = out_grad.reshape(rows, depth)
    weight = down_weight.reshape(2, hid, depth)

    sibling_weight = send(weight, 0, 0, 1)
    first, second = out_grad[0, 0], out_grad[0, 1]
    across = send(after(own, first, second), 0, 1, 0)
    low, high = [send(first, 1, 0, 0)], [send(second, -1, 0, 0)]
    far = send(low[0], 1, 0, 0), send(high[0], -1, 0, 0)
    low, high = (low[0], send(second, 1, 0, 0)), (send(first, -1, 0, 0), high[0])
    far_across = send(far[0], 0, 1, 0), send(far[1], 0, 1, 0)
    low_across, high_across = send(across, 1, 0, 0), send(across, -1, 0, 0)
    early = project([own, across, low, high, far], weight, sibling_weight)
    low_across = after(low_across, early[0])
    late = project([low_across, high_across, far_across], weight, sibling_weight)
    places = [(0, 0), (0, 1), (-1, 0), (1, 0), (2, 0), (-1, 1), (1, 1), (2, 1)]
    returned = []
    for i, ((dx, dy), made) in enumerate(zip(places, early + late)):
        if i >= len(early):
            made = after(made, returned[1])
        returned.append(send(made, dx, dy, 0) if dx or dy else made)
    table = np.array(
        [
            [
                expert_at(me // (NY * NC) - dx, me // NC % NY + dy, me % NC + dc)
                for dx, dy in places
                for dc in range(NC)
                for _ in range(16)
            ]
            for me in range(EXPERTS)
        ],
        np.int32,
    )
    marks = lax.dynamic_slice_in_dim(jnp.asarray(table), me, 1, 0)
    grad, part = token_math(
        marks, ids, probs, saved_input.reshape(rows, depth), [saved_hidden[0, s].reshape(tok * top, hid) for s in range(2)], returned
    )
    return grad.reshape(saved_hidden.shape), reduce_router(part, lax.rem(me, NC))[None]


def solution(mesh):
    in_specs = (
        P("pipe", None, "expert", None),
        P("pipe", None, "expert", None),
        P("pipe", None, "expert", None, None),
        P("pipe", None, "expert", None),
        P("pipe", None, "expert", None, None),
        P("pipe", None, None, None),
    )
    out_specs = (P("pipe", None, "expert", None, None), P("pipe", None, None, None))
    return jax.shard_map(local, mesh=mesh, in_specs=in_specs, out_specs=out_specs, check_vma=False)
```

```python
import functools

import jax
import jax.numpy as jnp
import numpy as np
from jax import lax
from jax.experimental import pallas as pl
from jax.experimental.pallas import tpu as pltpu
from jax.sharding import PartitionSpec as P

ROUTE_SCALE = 2.5
NX, NY, NC = 4, 2, 2
N_PIPE = 8
CUTS = 2
EXPERTS = NX * NY * NC
MIB = 1024 * 1024


def expert_at(x, y, c):
    return ((x % NX) * NY + y % NY) * NC + c % NC


def shift(dx, dy, dc):
    return [
        (expert_at(x, y, c), expert_at(x + dx, y + dy, c + dc))
        for x in range(NX)
        for y in range(NY)
        for c in range(NC)
    ]


def send(block, dx, dy, dc):
    return lax.ppermute(block, "expert", shift(dx, dy, dc))


def after(block, *earlier):
    return lax.optimization_barrier((block, *earlier))[0]


def send_mirror(block, dy, dc):
    route = [
        (p * EXPERTS + low, (N_PIPE - 1 - p) * EXPERTS + high)
        for p in range(N_PIPE)
        for low, high in shift(0, dy, dc)
    ]
    return lax.ppermute(block, ("pipe", "expert"), route)


def project_kernel(layout, depth_of, *refs):
    n, n_in = len(layout), sum(len(group) for group in layout)
    blocks, weights, outs = refs[:n_in], refs[n_in : n_in + NC], refs[n_in + NC : n_in + NC + n]
    tokens, held, stage, token_sem, weight_sem, out_sem = refs[n_in + NC + n :]
    tok = tokens.shape[0] // (2 * n)
    wide = held.shape[2]
    tiles = weights[0].shape[1] // wide

    def token_copy(slot, i):
        group = layout[i]
        if len(group) == 1:
            source = blocks[group[0]].at[pl.ds(slot * tok, tok)]
        else:
            source = blocks[group[slot]]
        target = tokens.at[pl.ds((slot * n + i) * tok, tok)]
        return pltpu.make_async_copy(source, target, token_sem.at[slot, i])

    def weight_copy(step, e):
        place = lax.rem(step, depth_of)
        return pltpu.make_async_copy(
            weights[e].at[step // tiles, pl.ds(lax.rem(step, tiles) * wide, wide)],
            held.at[place, e],
            weight_sem.at[place, e],
        )

    def out_copy(slot, i):
        return pltpu.make_async_copy(
            stage.at[slot, i], outs[i].at[:, pl.ds(slot * tok, tok)], out_sem.at[slot, i]
        )

    for i in range(n):
        token_copy(0, i).start()
    for e in range(NC):
        weight_copy(0, e).start()
    for i in range(n):
        token_copy(1, i).start()
    for step in range(1, depth_of):
        for e in range(NC):
            weight_copy(step, e).start()

    def body(step, carry):
        slot, tile = step // tiles, lax.rem(step, tiles)
        for s in range(2):

            @pl.when(step == s * tiles)
            def _(s=s):
                for i in range(n):
                    token_copy(s, i).wait()

        rows = pl.ds(pl.multiple_of(slot * n * tok, tok), n * tok)
        cols = pl.ds(pl.multiple_of(tile * wide, wide), wide)
        for e in range(NC):
            weight_copy(step, e).wait()
            made = lax.dot_general(
                tokens[rows, :],
                held[lax.rem(step, depth_of), e],
                (((1,), (1,)), ((), ())),
                preferred_element_type=jnp.float32,
            ).astype(jnp.bfloat16)
            for i in range(n):
                stage[slot, i, e, :, cols] = made[i * tok : (i + 1) * tok]

            @pl.when(step + depth_of < 2 * tiles)
            def _(e=e):
                weight_copy(step + depth_of, e).start()

        for s in range(2):

            @pl.when(step == (s + 1) * tiles - 1)
            def _(s=s):
                for i in range(n):
                    out_copy(s, i).start()

        return carry

    lax.fori_loop(0, 2 * tiles, body, 0)
    for s in range(2):
        for i in range(n):
            out_copy(s, i).wait()


def project(shards, own, sibling):
    layout, blocks = [], []
    for shard in shards:
        shard = shard if isinstance(shard, tuple) else (shard,)
        layout.append(tuple(range(len(blocks), len(blocks) + len(shard))))
        blocks += shard
    n = len(shards)
    _, hid, depth = own.shape
    tok = max(b.shape[0] for b in blocks) // 2
    wide, depth_of = 512, 2
    anywhere = pl.BlockSpec(memory_space=pl.ANY)
    return pl.pallas_call(
        functools.partial(project_kernel, layout, depth_of),
        in_specs=[anywhere] * (len(blocks) + NC),
        out_specs=[anywhere] * n,
        out_shape=[jax.ShapeDtypeStruct((NC, 2 * tok, hid), jnp.bfloat16)] * n,
        scratch_shapes=[
            pltpu.VMEM((2 * n * tok, depth), jnp.bfloat16),
            pltpu.VMEM((depth_of, NC, wide, depth), jnp.bfloat16),
            pltpu.VMEM((2, n, NC, tok, hid), jnp.bfloat16),
            pltpu.SemaphoreType.DMA((2, n)),
            pltpu.SemaphoreType.DMA((depth_of, NC)),
            pltpu.SemaphoreType.DMA((2, n)),
        ],
        compiler_params=pltpu.CompilerParams(vmem_limit_bytes=40 * MIB),
        cost_estimate=pl.CostEstimate(
            flops=8 * n * tok * depth * hid,
            bytes_accessed=8 * hid * depth + 4 * n * tok * (depth + 2 * hid),
            transcendentals=0,
        ),
    )(*blocks, own, sibling)


def token_kernel(n, source, ids, probs, inputs, *refs):
    hidden, returned, (grad, part) = refs[:2], refs[2 : n + 2], refs[n + 2 : n + 4]
    grad_out, logits, out_sem = refs[n + 4 :]
    chunks, tok, top = grad_out.shape[0], 16, 8
    half = inputs.shape[0] // 2
    span = 2 * half // chunks

    def out_copy(q):
        target = grad.at[pl.ds(q * span * top, span * top)]
        return pltpu.make_async_copy(grad_out.at[q], target, out_sem.at[q])

    shape = (tok * top, EXPERTS * tok)
    mine = lax.broadcasted_iota(jnp.int32, shape, 0) // top == lax.broadcasted_iota(
        jnp.int32, shape, 1
    ) % tok
    for q in range(chunks):
        for g in range(span // tok):
            first = q * span + g * tok
            at = slice(g * tok * top, (g + 1) * tok * top)
            slot, within = first // half, first % half * top
            rows = jnp.concatenate(
                [r[e, first : first + tok, :] for r in returned for e in range(NC)], axis=0
            )
            routes = ids[first * top : (first + tok) * top, :]
            pick = jnp.where(jnp.logical_and(mine, routes == source[...]), 1.0, 0.0)
            back = jnp.dot(pick.astype(jnp.bfloat16), rows, preferred_element_type=jnp.float32)
            saved = hidden[slot][within : within + tok * top, :].astype(jnp.float32)
            dgate = jnp.sum(saved * back, axis=1, keepdims=True).reshape(tok, top, 1)
            member = routes.reshape(tok, top, 1) == lax.broadcasted_iota(
                jnp.int32, (tok, top, EXPERTS), 2
            )
            chosen = jnp.sum(
                jnp.where(member, probs[first : first + tok, :][:, None, :], 0.0),
                axis=2,
                keepdims=True,
            )
            total = jnp.sum(chosen, axis=1, keepdims=True)
            share = chosen / total
            weights = (ROUTE_SCALE * share).reshape(tok * top, 1)
            grad_out[q, at, :] = (weights * back).astype(jnp.bfloat16)
            centred = dgate - jnp.sum(share * dgate, axis=1, keepdims=True)
            selected = ROUTE_SCALE / total * centred * chosen * (1.0 - chosen)
            logits[first : first + tok, :] = jnp.sum(jnp.where(member, selected, 0.0), axis=1)
        out_copy(q).start()

    for s in range(2):
        logit = logits[s * half : (s + 1) * half, :]
        high = logit.astype(jnp.bfloat16)
        low = (logit - high.astype(jnp.float32)).astype(jnp.bfloat16)
        over = (((0,), (0,)), ((), ()))
        values = inputs[s * half : (s + 1) * half, :]
        made = lax.dot_general(high, values, over, preferred_element_type=jnp.float32)
        part[s] = made + lax.dot_general(low, values, over, preferred_element_type=jnp.float32)
    for q in range(chunks):
        out_copy(q).wait()


def token_math(source, ids, probs, inputs, hidden, returned):
    rows, depth = inputs.shape
    top, hid = 8, hidden[0].shape[1]
    n, chunks = len(returned), 4
    span = rows // chunks
    inside = pl.BlockSpec(memory_space=pltpu.VMEM)
    anywhere = pl.BlockSpec(memory_space=pl.ANY)
    return pl.pallas_call(
        functools.partial(token_kernel, n),
        in_specs=[inside] * (6 + n),
        out_specs=[anywhere, inside],
        out_shape=[
            jax.ShapeDtypeStruct((rows * top, hid), jnp.bfloat16),
            jax.ShapeDtypeStruct((2, EXPERTS, depth), jnp.float32),
        ],
        scratch_shapes=[
            pltpu.VMEM((chunks, span * top, hid), jnp.bfloat16),
            pltpu.VMEM((rows, EXPERTS), jnp.float32),
            pltpu.SemaphoreType.DMA((chunks,)),
        ],
        compiler_params=pltpu.CompilerParams(vmem_limit_bytes=16 * MIB),
        cost_estimate=pl.CostEstimate(
            flops=2 * rows * top * hid * EXPERTS * 16,
            bytes_accessed=2 * rows * hid * (2 * top + EXPERTS),
            transcendentals=0,
        ),
    )(source, ids, probs, inputs, *hidden, *returned)


def reduce_router(part, core):
    wide = jnp.float32
    narrow = jnp.bfloat16
    first = core == 0
    keep = jnp.where(first, part[0], part[1])
    give = jnp.where(first, part[1], part[0])
    pair = (keep + send(give, 0, 0, 1)).astype(narrow)
    low, high, far = send(pair, 1, 0, 0), send(pair, -1, 0, 0), send(pair, 2, 0, 0)
    line = (
        (pair.astype(wide) + far.astype(wide)) + (low.astype(wide) + high.astype(wide))
    ).astype(narrow)
    other = send(line, 0, 1, 0)
    mirror, mirror_other = send_mirror(line, 0, 1), send_mirror(line, 1, 1)
    total = (line.astype(wide) + other.astype(wide)) + (
        mirror.astype(wide) + mirror_other.astype(wide)
    )
    sibling = send(total, 0, 0, 1)
    here = jnp.arange(2)[:, None, None] == core
    return jnp.where(here, total[None], sibling[None])


def local(out_grad, saved_input, saved_hidden, expert_ids, down_weight, router_weight):
    tok, depth = out_grad.shape[2:]
    top, hid = saved_hidden.shape[3:]
    rows = 2 * tok
    me = lax.axis_index("expert")

    logits = jnp.einsum(
        "std,sed->ste", saved_input[0], router_weight[0], preferred_element_type=jnp.float32
    )
    probs = jax.nn.sigmoid(logits).reshape(rows, EXPERTS)
    ids = expert_ids.reshape(rows * top, 1)

    own = out_grad.reshape(rows, depth)
    weight = down_weight.reshape(2, hid, depth)

    across = send(own, 0, 1, 0)
    sibling_weight = send(weight, 0, 0, 1)
    first, second = out_grad[0, 0], out_grad[0, 1]
    low, high = [send(first, 1, 0, 0)], [send(second, -1, 0, 0)]
    far = send(low[0], 1, 0, 0), send(high[0], -1, 0, 0)
    low, high = (low[0], send(second, 1, 0, 0)), (send(first, -1, 0, 0), high[0])
    far_across = send(far[0], 0, 1, 0), send(far[1], 0, 1, 0)
    low_across, high_across = send(across, 1, 0, 0), send(across, -1, 0, 0)
    early = project([(first, second), across, low, high, far], weight, sibling_weight)
    low_across = after(low_across, early[0])
    late = project([low_across, high_across, far_across], weight, sibling_weight)
    places = [(0, 0), (0, 1), (-1, 0), (1, 0), (2, 0), (-1, 1), (1, 1), (2, 1)]
    returned = []
    for i, ((dx, dy), made) in enumerate(zip(places, early + late)):
        if i >= len(early):
            made = after(made, returned[1])
        returned.append(send(made, dx, dy, 0) if dx or dy else made)
    table = np.array(
        [
            [
                expert_at(me // (NY * NC) - dx, me // NC % NY + dy, me % NC + dc)
                for dx, dy in places
                for dc in range(NC)
                for _ in range(16)
            ]
            for me in range(EXPERTS)
        ],
        np.int32,
    )
    marks = lax.dynamic_slice_in_dim(jnp.asarray(table), me, 1, 0)
    grad, part = token_math(
        marks, ids, probs, saved_input.reshape(rows, depth), [saved_hidden[0, s].reshape(tok * top, hid) for s in range(2)], returned
    )
    return grad.reshape(saved_hidden.shape), reduce_router(part, lax.rem(me, NC))[None]


def solution(mesh):
    in_specs = (
        P("pipe", None, "expert", None),
        P("pipe", None, "expert", None),
        P("pipe", None, "expert", None, None),
        P("pipe", None, "expert", None),
        P("pipe", None, "expert", None, None),
        P("pipe", None, None, None),
    )
    out_specs = (P("pipe", None, "expert", None, None), P("pipe", None, None, None))
    return jax.shard_map(local, mesh=mesh, in_specs=in_specs, out_specs=out_specs, check_vma=False)
```

```python
import functools

import jax
import jax.numpy as jnp
import numpy as np
from jax import lax
from jax.experimental import pallas as pl
from jax.experimental.pallas import tpu as pltpu
from jax.sharding import PartitionSpec as P

ROUTE_SCALE = 2.5
NX, NY, NC = 4, 2, 2
N_PIPE = 8
CUTS = 2
EXPERTS = NX * NY * NC
MIB = 1024 * 1024


def expert_at(x, y, c):
    return ((x % NX) * NY + y % NY) * NC + c % NC


def shift(dx, dy, dc):
    return [
        (expert_at(x, y, c), expert_at(x + dx, y + dy, c + dc))
        for x in range(NX)
        for y in range(NY)
        for c in range(NC)
    ]


def send(block, dx, dy, dc):
    return lax.ppermute(block, "expert", shift(dx, dy, dc))


def after(block, *earlier):
    return lax.optimization_barrier((block, *earlier))[0]


def send_mirror(block, dy, dc):
    route = [
        (p * EXPERTS + low, (N_PIPE - 1 - p) * EXPERTS + high)
        for p in range(N_PIPE)
        for low, high in shift(0, dy, dc)
    ]
    return lax.ppermute(block, ("pipe", "expert"), route)


def project_kernel(layout, depth_of, *refs):
    n, n_in = len(layout), sum(len(group) for group in layout)
    blocks, weights, outs = refs[:n_in], refs[n_in : n_in + NC], refs[n_in + NC : n_in + NC + n]
    tokens, held, stage, token_sem, weight_sem, out_sem = refs[n_in + NC + n :]
    tok = tokens.shape[0] // (2 * n)
    wide = held.shape[2]
    tiles = weights[0].shape[1] // wide

    def token_copy(slot, i):
        group = layout[i]
        if len(group) == 1:
            source = blocks[group[0]].at[pl.ds(slot * tok, tok)]
        else:
            source = blocks[group[slot]]
        target = tokens.at[pl.ds((slot * n + i) * tok, tok)]
        return pltpu.make_async_copy(source, target, token_sem.at[slot, i])

    def weight_copy(step, e):
        place = lax.rem(step, depth_of)
        return pltpu.make_async_copy(
            weights[e].at[step // tiles, pl.ds(lax.rem(step, tiles) * wide, wide)],
            held.at[place, e],
            weight_sem.at[place, e],
        )

    def out_copy(slot, i):
        return pltpu.make_async_copy(
            stage.at[slot, i], outs[i].at[:, pl.ds(slot * tok, tok)], out_sem.at[slot, i]
        )

    for i in range(n):
        token_copy(0, i).start()
    for e in range(NC):
        weight_copy(0, e).start()
    for i in range(n):
        token_copy(1, i).start()
    for step in range(1, depth_of):
        for e in range(NC):
            weight_copy(step, e).start()

    def body(step, carry):
        slot, tile = step // tiles, lax.rem(step, tiles)
        for s in range(2):

            @pl.when(step == s * tiles)
            def _(s=s):
                for i in range(n):
                    token_copy(s, i).wait()

        rows = pl.ds(pl.multiple_of(slot * n * tok, tok), n * tok)
        cols = pl.ds(pl.multiple_of(tile * wide, wide), wide)
        for e in range(NC):
            weight_copy(step, e).wait()
            made = lax.dot_general(
                tokens[rows, :],
                held[lax.rem(step, depth_of), e],
                (((1,), (1,)), ((), ())),
                preferred_element_type=jnp.float32,
            ).astype(jnp.bfloat16)
            for i in range(n):
                stage[slot, i, e, :, cols] = made[i * tok : (i + 1) * tok]

            @pl.when(step + depth_of < 2 * tiles)
            def _(e=e):
                weight_copy(step + depth_of, e).start()

        for s in range(2):

            @pl.when(step == (s + 1) * tiles - 1)
            def _(s=s):
                for i in range(n):
                    out_copy(s, i).start()

        return carry

    lax.fori_loop(0, 2 * tiles, body, 0)
    for s in range(2):
        for i in range(n):
            out_copy(s, i).wait()


def project(shards, own, sibling):
    layout, blocks = [], []
    for shard in shards:
        shard = shard if isinstance(shard, tuple) else (shard,)
        layout.append(tuple(range(len(blocks), len(blocks) + len(shard))))
        blocks += shard
    n = len(shards)
    _, hid, depth = own.shape
    tok = blocks[0].shape[0] // 2
    wide, depth_of = 512, 2
    anywhere = pl.BlockSpec(memory_space=pl.ANY)
    return pl.pallas_call(
        functools.partial(project_kernel, layout, depth_of),
        in_specs=[anywhere] * (len(blocks) + NC),
        out_specs=[anywhere] * n,
        out_shape=[jax.ShapeDtypeStruct((NC, 2 * tok, hid), jnp.bfloat16)] * n,
        scratch_shapes=[
            pltpu.VMEM((2 * n * tok, depth), jnp.bfloat16),
            pltpu.VMEM((depth_of, NC, wide, depth), jnp.bfloat16),
            pltpu.VMEM((2, n, NC, tok, hid), jnp.bfloat16),
            pltpu.SemaphoreType.DMA((2, n)),
            pltpu.SemaphoreType.DMA((depth_of, NC)),
            pltpu.SemaphoreType.DMA((2, n)),
        ],
        compiler_params=pltpu.CompilerParams(vmem_limit_bytes=48 * MIB),
        cost_estimate=pl.CostEstimate(
            flops=8 * n * tok * depth * hid,
            bytes_accessed=8 * hid * depth + 4 * n * tok * (depth + 2 * hid),
            transcendentals=0,
        ),
    )(*blocks, own, sibling)


def token_kernel(n, source, ids, probs, inputs, *refs):
    hidden, returned, (grad, part) = refs[:2], refs[2 : n + 2], refs[n + 2 : n + 4]
    grad_out, logits, out_sem = refs[n + 4 :]
    chunks, tok, top = grad_out.shape[0], 16, 8
    half = inputs.shape[0] // 2
    span = 2 * half // chunks

    def out_copy(q):
        target = grad.at[pl.ds(q * span * top, span * top)]
        return pltpu.make_async_copy(grad_out.at[q], target, out_sem.at[q])

    shape = (tok * top, EXPERTS * tok)
    mine = lax.broadcasted_iota(jnp.int32, shape, 0) // top == lax.broadcasted_iota(
        jnp.int32, shape, 1
    ) % tok
    for q in range(chunks):
        for g in range(span // tok):
            first = q * span + g * tok
            at = slice(g * tok * top, (g + 1) * tok * top)
            slot, within = first // half, first % half * top
            rows = jnp.concatenate(
                [r[e, first : first + tok, :] for r in returned for e in range(NC)], axis=0
            )
            routes = ids[first * top : (first + tok) * top, :]
            pick = jnp.where(jnp.logical_and(mine, routes == source[...]), 1.0, 0.0)
            back = jnp.dot(pick.astype(jnp.bfloat16), rows, preferred_element_type=jnp.float32)
            saved = hidden[slot][within : within + tok * top, :].astype(jnp.float32)
            dgate = jnp.sum(saved * back, axis=1, keepdims=True).reshape(tok, top, 1)
            member = routes.reshape(tok, top, 1) == lax.broadcasted_iota(
                jnp.int32, (tok, top, EXPERTS), 2
            )
            chosen = jnp.sum(
                jnp.where(member, probs[first : first + tok, :][:, None, :], 0.0),
                axis=2,
                keepdims=True,
            )
            total = jnp.sum(chosen, axis=1, keepdims=True)
            share = chosen / total
            weights = (ROUTE_SCALE * share).reshape(tok * top, 1)
            grad_out[q, at, :] = (weights * back).astype(jnp.bfloat16)
            centred = dgate - jnp.sum(share * dgate, axis=1, keepdims=True)
            selected = ROUTE_SCALE / total * centred * chosen * (1.0 - chosen)
            logits[first : first + tok, :] = jnp.sum(jnp.where(member, selected, 0.0), axis=1)
        out_copy(q).start()

    for s in range(2):
        logit = logits[s * half : (s + 1) * half, :]
        high = logit.astype(jnp.bfloat16)
        low = (logit - high.astype(jnp.float32)).astype(jnp.bfloat16)
        over = (((0,), (0,)), ((), ()))
        values = inputs[s * half : (s + 1) * half, :]
        both = jnp.concatenate([high, low], axis=1)
        made = lax.dot_general(both, values, over, preferred_element_type=jnp.float32)
        part[s] = made[:EXPERTS] + made[EXPERTS:]
    for q in range(chunks):
        out_copy(q).wait()


def token_math(source, ids, probs, inputs, hidden, returned):
    rows, depth = inputs.shape
    top, hid = 8, hidden[0].shape[1]
    n, chunks = len(returned), 4
    span = rows // chunks
    inside = pl.BlockSpec(memory_space=pltpu.VMEM)
    anywhere = pl.BlockSpec(memory_space=pl.ANY)
    return pl.pallas_call(
        functools.partial(token_kernel, n),
        in_specs=[inside] * (6 + n),
        out_specs=[anywhere, inside],
        out_shape=[
            jax.ShapeDtypeStruct((rows * top, hid), jnp.bfloat16),
            jax.ShapeDtypeStruct((2, EXPERTS, depth), jnp.float32),
        ],
        scratch_shapes=[
            pltpu.VMEM((chunks, span * top, hid), jnp.bfloat16),
            pltpu.VMEM((rows, EXPERTS), jnp.float32),
            pltpu.SemaphoreType.DMA((chunks,)),
        ],
        compiler_params=pltpu.CompilerParams(vmem_limit_bytes=16 * MIB),
        cost_estimate=pl.CostEstimate(
            flops=2 * rows * top * hid * EXPERTS * 16,
            bytes_accessed=2 * rows * hid * (2 * top + EXPERTS),
            transcendentals=0,
        ),
    )(source, ids, probs, inputs, *hidden, *returned)


def reduce_router(part, core):
    wide = jnp.float32
    narrow = jnp.bfloat16
    first = core == 0
    keep = jnp.where(first, part[0], part[1])
    give = jnp.where(first, part[1], part[0])
    pair = (keep + send(give, 0, 0, 1)).astype(narrow)
    low, high, far = send(pair, 1, 0, 0), send(pair, -1, 0, 0), send(pair, 2, 0, 0)
    line = (
        (pair.astype(wide) + far.astype(wide)) + (low.astype(wide) + high.astype(wide))
    ).astype(narrow)
    other = send(line, 0, 1, 0)
    mirror, mirror_other = send_mirror(line, 0, 1), send_mirror(line, 1, 1)
    total = (line.astype(wide) + other.astype(wide)) + (
        mirror.astype(wide) + mirror_other.astype(wide)
    )
    sibling = send(total, 0, 0, 1)
    return jnp.stack([jnp.where(first, total, sibling), jnp.where(first, sibling, total)])


def local(out_grad, saved_input, saved_hidden, expert_ids, down_weight, router_weight):
    tok, depth = out_grad.shape[2:]
    top, hid = saved_hidden.shape[3:]
    rows = 2 * tok
    me = lax.axis_index("expert")

    logits = jnp.einsum(
        "std,sed->ste", saved_input[0], router_weight[0], preferred_element_type=jnp.float32
    )
    probs = jax.nn.sigmoid(logits).reshape(rows, EXPERTS)
    ids = expert_ids.reshape(rows * top, 1)

    own = out_grad.reshape(rows, depth)
    weight = down_weight.reshape(2, hid, depth)

    across = send(own, 0, 1, 0)
    sibling_weight = send(weight, 0, 0, 1)
    first, second = out_grad[0, 0], out_grad[0, 1]
    low, high = [send(first, 1, 0, 0)], [send(second, -1, 0, 0)]
    far = send(low[0], 1, 0, 0), send(high[0], -1, 0, 0)
    low, high = (low[0], send(second, 1, 0, 0)), (send(first, -1, 0, 0), high[0])
    far_across = send(far[0], 0, 1, 0), send(far[1], 0, 1, 0)
    low_across, high_across = send(across, 1, 0, 0), send(across, -1, 0, 0)
    early = project([own, across, low, high, far], weight, sibling_weight)
    low_across = after(low_across, early[0])
    late = project([low_across, high_across, far_across], weight, sibling_weight)
    places = [(0, 0), (0, 1), (-1, 0), (1, 0), (2, 0), (-1, 1), (1, 1), (2, 1)]
    returned = []
    for i, ((dx, dy), made) in enumerate(zip(places, early + late)):
        if i >= len(early):
            made = after(made, returned[1])
        returned.append(send(made, dx, dy, 0) if dx or dy else made)
    table = np.array(
        [
            [
                expert_at(me // (NY * NC) - dx, me // NC % NY + dy, me % NC + dc)
                for dx, dy in places
                for dc in range(NC)
                for _ in range(16)
            ]
            for me in range(EXPERTS)
        ],
        np.int32,
    )
    marks = lax.dynamic_slice_in_dim(jnp.asarray(table), me, 1, 0)
    grad, part = token_math(
        marks, ids, probs, saved_input.reshape(rows, depth), [saved_hidden[0, s].reshape(tok * top, hid) for s in range(2)], returned
    )
    return grad.reshape(saved_hidden.shape), reduce_router(part, lax.rem(me, NC))[None]


def solution(mesh):
    in_specs = (
        P("pipe", None, "expert", None),
        P("pipe", None, "expert", None),
        P("pipe", None, "expert", None, None),
        P("pipe", None, "expert", None),
        P("pipe", None, "expert", None, None),
        P("pipe", None, None, None),
    )
    out_specs = (P("pipe", None, "expert", None, None), P("pipe", None, None, None))
    return jax.shard_map(local, mesh=mesh, in_specs=in_specs, out_specs=out_specs, check_vma=False)
```
